128 devices in a mesh: corpus: 16 (over z, x_lo, core), group: 8 (over x_hi, y).
Axes of the slice: x: 4 (x_hi: 2, x_lo: 2; x = x_hi * 2 + x_lo), y: 4, z: 4, core: 2. Of those that a mesh axis runs over, the one named last changes fastest.
Arguments:
- queries: bfloat16 [1024, 32768], P('corpus', 'group'), may hold values from -6 to 6
- precond: bfloat16 [8, 4096, 4096], P('group', 'corpus'), may hold values from -0.09375 to 0.09375
- documents: bfloat16 [24576, 32768], P('corpus', 'group'), may hold values from -6 to 6
Outputs:
- scores: float32 [1024, 24576], P('group', 'corpus')
The draws below stay inside these ranges and needn't reach their ends.
All inputs are finite; a program needn't handle non-finite values.
Results may differ from the reference program's by a relative error of at most 0.0029.
Values may be sent and summed in bfloat16 or wider, within the bound.
No kernel may reach another device: no remote copies, remote signals or barrier semaphores. Data moves between devices by JAX's collectives and lax.ppermute only.
A program may use at most 128 MiB of HBM per device.

```python
import jax
import jax.numpy as jnp

FG = 4096
GROUPS = 8
QUERIES = 1024
DOCS = 24576


def steps_of(stream_key, dims, split, least, largest):
    gain = 1.0
    for dim, shards_of in split:
        heights = jax.random.uniform(jax.random.fold_in(jax.random.fold_in(stream_key, 6), dim), (shards_of,), jnp.float32, least / len(split), largest / len(split))
        gain = gain * jnp.repeat(jnp.exp(heights), dims[dim] // shards_of).reshape((-1,) + (1,) * (len(dims) - 1 - dim))
    return gain


def scatter_about(key, shape, scale, most, pieces=(), kind=jnp.bfloat16):
    result = scale * jax.random.normal(key, shape, jnp.float32)
    if pieces:
        result = result * steps_of(key, shape, pieces, -0.22, 0.18)
    return jnp.clip(result, -most, most).astype(kind)


def setup_inputs(seed: int = 0) -> dict:
    seeds = jax.random.split(jax.random.key(seed), 4)
    return {
        "queries": scatter_about(seeds[0], (QUERIES, GROUPS * FG), 1.0, 6.0, ((0, 16), (1, 8))),
        "precond": scatter_about(seeds[1], (GROUPS, FG, FG), FG ** -0.5, 0.09375, ((0, 8), (1, 16))),
        "documents": scatter_about(seeds[2], (DOCS, GROUPS * FG), 1.0, 6.0, ((0, 16), (1, 8))),
    }


def reference(queries, precond, documents):
    total = jnp.zeros((queries.shape[0], documents.shape[0]), jnp.float32)
    for g in range(GROUPS):
        query_part = queries[:, g * FG:(g + 1) * FG]
        doc_part = documents[:, g * FG:(g + 1) * FG]
        conditioned = jnp.dot(query_part, precond[g], preferred_element_type=jnp.float32).astype(jnp.bfloat16)
        total = total + jnp.dot(conditioned, doc_part.T, preferred_element_type=jnp.float32)
    return total / jnp.sqrt(jnp.float32(GROUPS * FG))
```

```python
import functools

import jax
import jax.numpy as jnp
from jax import lax
from jax.experimental import pallas as pl
from jax.experimental.pallas import tpu as pltpu
from jax.sharding import PartitionSpec as P

NZ, NX, NC, NH, NY = 4, 2, 2, 2, 4
CHIPS = NZ * NX
GROUP = NH * NY
ROLES = ((0, 0), (-1, 0), (1, 0), (2, 0), (0, 1), (-1, 1), (1, 1), (2, 1))


def corpus_perm(move):
    pairs = []
    for z in range(NZ):
        for x in range(NX):
            for c in range(NC):
                dz, dx, dc = move(1 - 2 * c)
                to = ((z + dz) % NZ, (x + dx) % NX, (c + dc) % NC)
                pairs.append(((z * NX + x) * NC + c, (to[0] * NX + to[1]) * NC + to[2]))
    return pairs


def group_perm(dh, dy):
    return [(h * NY + y, (h + dh) % NH * NY + (y + dy) % NY) for h in range(NH) for y in range(NY)]


AHEAD = corpus_perm(lambda d: (d, 0, 0))
BACK = corpus_perm(lambda d: (-d, 0, 0))
CROSS = corpus_perm(lambda d: (0, 1, 0))
CORE = corpus_perm(lambda d: (0, 0, 1))
SAME_CORE = [[chip * NC + c for chip in range(CHIPS)] for c in range(NC)]


def gather_pieces(own):
    go = functools.partial(lax.ppermute, axis_name="corpus")
    cross = go(own, perm=CROSS)
    behind = go(own, perm=AHEAD)
    ahead = go(own, perm=BACK)
    cross_behind = go(cross, perm=AHEAD)
    far = go(behind, perm=AHEAD)
    cross_ahead = go(ahead, perm=CROSS)
    cross_far = go(cross_behind, perm=AHEAD)
    return [own, behind, ahead, far, cross, cross_behind, cross_ahead, cross_far]


def chip_of(direction):
    place = lax.axis_index("corpus")
    z, x = place // (NX * NC), place // NC % NX
    return [((z + dz * direction + NZ) % NZ) * NX + (x + dx) % NX for dz, dx in ROLES]


def condition_kernel(place, *refs):
    pieces, weights, own, other, rows = refs[:CHIPS], *refs[CHIPS:]
    half = pieces[0].shape[0] // 2
    total = own.shape[0]
    for i, piece in enumerate(pieces):
        start = pl.multiple_of(place[i] * half, half)
        rows[pl.ds(start, half), :] = piece[:half, :]
        rows[pl.ds(total + start, half), :] = piece[half:, :]
    step = min(256, total)

    @pl.loop(0, total // step)
    def _(i):
        at = pl.ds(pl.multiple_of(i * step, step), step)
        own[at, :] = jnp.dot(rows[at, :], weights[...], preferred_element_type=jnp.float32)

    @pl.loop(0, total // step)
    def _(i):
        at = pl.ds(pl.multiple_of(i * step, step), step)
        off = pl.ds(pl.multiple_of(total + i * step, step), step)
        other[at, :] = jnp.dot(rows[off, :], weights[...], preferred_element_type=jnp.float32)


def condition(place, pieces, weights):
    rows, depth = pieces[0].shape
    wide = weights.shape[1]
    total = rows // 2 * CHIPS
    whole = pl.BlockSpec(memory_space=pltpu.VMEM)
    return pl.pallas_call(
        condition_kernel,
        out_shape=[jax.ShapeDtypeStruct((total, wide), jnp.float32)] * 2,
        in_specs=[pl.BlockSpec(memory_space=pltpu.SMEM)] + [whole] * (CHIPS + 1),
        out_specs=[whole] * 2,
        scratch_shapes=[pltpu.VMEM((2 * total, depth), jnp.bfloat16)],
        compiler_params=pltpu.CompilerParams(vmem_limit_bytes=32 * 2**20),
        cost_estimate=pl.CostEstimate(flops=4 * total * depth * wide, bytes_accessed=2**23, transcendentals=0),
    )(place, *pieces, weights)


def score_kernel(chips, *refs):
    pieces, docs = refs[:CHIPS], refs[CHIPS]
    outs, (acc, piece) = refs[CHIPS + 1 : -2], refs[-2:]
    k = pl.program_id(0)
    for i, ref in enumerate(pieces):

        @pl.when(k == i)
        def _():
            piece[...] = ref[...]

    step = 256
    steps = docs.shape[0] // step

    def add(first):
        @pl.loop(0, steps)
        def _(i):
            at = pl.ds(pl.multiple_of(i * step, step), step)
            part = lax.dot_general(
                piece[...], docs[at, :], (((1,), (1,)), ((), ())), preferred_element_type=jnp.float32
            )
            acc[:, at] = part if first else acc[:, at] + part

    @pl.when(k == 0)
    def _():
        add(True)

    @pl.when(k > 0)
    def _():
        add(False)

    @pl.when(k == CHIPS - 1)
    def _():
        tall = outs[0].shape[0]
        for i, out in enumerate(outs):
            out[...] = acc[i * tall : (i + 1) * tall, :].astype(out.dtype)


def score(chips, pieces, docs):
    rows, wide = pieces[0].shape
    n_docs = docs.shape[0]
    tall = rows // NY
    whole = pl.BlockSpec(pieces[0].shape, lambda k, chips: (0, 0))
    out = pl.BlockSpec((tall, n_docs), lambda k, chips: (0, 0))
    return pl.pallas_call(
        score_kernel,
        out_shape=[
            jax.ShapeDtypeStruct((tall, n_docs), jnp.bfloat16 if i else jnp.float32) for i in range(NY)
        ],
        grid_spec=pltpu.PrefetchScalarGridSpec(
            num_scalar_prefetch=1,
            grid=(CHIPS,),
            in_specs=[whole] * CHIPS + [pl.BlockSpec((n_docs, wide), lambda k, chips: (0, chips[k]))],
            out_specs=[out] * NY,
            scratch_shapes=[
                pltpu.VMEM((rows, n_docs), jnp.float32),
                pltpu.VMEM((rows, wide), jnp.bfloat16),
            ],
        ),
        compiler_params=pltpu.CompilerParams(
            dimension_semantics=("arbitrary",), vmem_limit_bytes=40 * 2**20
        ),
        cost_estimate=pl.CostEstimate(
            flops=2 * rows * n_docs * wide * CHIPS, bytes_accessed=n_docs * wide * CHIPS * 2, transcendentals=0
        ),
    )(chips, *pieces, docs)


def reduce_scores(parts):
    own, ahead, far, back = parts
    go = functools.partial(lax.ppermute, axis_name="group")
    got = [go(ahead, perm=group_perm(0, 1)), go(back, perm=group_perm(0, -1)), go(far, perm=group_perm(0, 2))]
    total = own
    for part in got:
        total = total + part.astype(jnp.float32)
    half = total.shape[0] // NH
    sent = go(total[half:].astype(jnp.bfloat16), perm=group_perm(1, 0))
    return total[:half] + sent.astype(jnp.float32)


def local(queries, precond, documents):
    rows, feat = queries.shape
    core = lax.axis_index("corpus") % NC
    direction = 1 - 2 * core
    h, y = lax.axis_index("group") // NY, lax.axis_index("group") % NY

    split = queries.reshape(rows, CHIPS, NC, feat // (CHIPS * NC))
    mine, theirs = [
        lax.dynamic_index_in_dim(split, i, 2, keepdims=False).reshape(rows, feat // NC)
        for i in (core, 1 - core)
    ]
    query_piece = jnp.concatenate([mine, lax.ppermute(theirs, "corpus", CORE)], axis=0)
    query_pieces = gather_pieces(query_piece)
    weights = lax.all_to_all(precond[0], "corpus", 1, 0, tiled=True, axis_index_groups=SAME_CORE)

    chips = jnp.stack(chip_of(direction))
    chips_other = jnp.stack(chip_of(-direction))
    place = (chips % NY - y + NY) % NY * NH + (chips // NY - h + NH) % NH
    own, other = condition(place, query_pieces, weights)
    conditioned = (own + lax.ppermute(other, "corpus", CORE)).astype(jnp.bfloat16)

    pieces = gather_pieces(conditioned)
    pieces_other = [lax.ppermute(piece, "corpus", CORE) for piece in pieces]
    mine = reduce_scores(score(chips, pieces, documents))
    theirs = reduce_scores(score(chips_other, pieces_other, documents))
    first = core == 0
    scores = jnp.concatenate([jnp.where(first, mine, theirs), jnp.where(first, theirs, mine)], axis=0)
    return scores / jnp.sqrt(jnp.float32(GROUP * feat))


def solution(mesh):
    placed = (P("corpus", "group"), P("group", "corpus", None), P("corpus", "group"))
    return jax.shard_map(
        local, mesh=mesh, in_specs=placed, out_specs=P("group", "corpus"), check_vma=False
    )
```

```python
import functools

import jax
import jax.numpy as jnp
from jax import lax
from jax.experimental import pallas as pl
from jax.experimental.pallas import tpu as pltpu
from jax.sharding import PartitionSpec as P

NZ, NX, NC, NH, NY = 4, 2, 2, 2, 4
CHIPS = NZ * NX
GROUP = NH * NY
ROLES = ((0, 0), (0, 1), (-1, 0), (1, 0), (-1, 1), (2, 0), (1, 1), (2, 1))
STAGES = ((0, 4), (4, 7), (7, 8))


def corpus_perm(move):
    pairs = []
    for z in range(NZ):
        for x in range(NX):
            for c in range(NC):
                dz, dx, dc = move(1 - 2 * c)
                to = ((z + dz) % NZ, (x + dx) % NX, (c + dc) % NC)
                pairs.append(((z * NX + x) * NC + c, (to[0] * NX + to[1]) * NC + to[2]))
    return pairs


def group_perm(dh, dy):
    return [(h * NY + y, (h + dh) % NH * NY + (y + dy) % NY) for h in range(NH) for y in range(NY)]


AHEAD = corpus_perm(lambda d: (d, 0, 0))
BACK = corpus_perm(lambda d: (-d, 0, 0))
CROSS = corpus_perm(lambda d: (0, 1, 0))
CORE = corpus_perm(lambda d: (0, 0, 1))


CHUNKS = 2
STEP = 512
SCOPED = 16 * 2**20
ANY_SPEC = pl.BlockSpec(memory_space=pl.ANY)
HBM_SPEC = pl.BlockSpec(memory_space=pltpu.HBM)
VMEM_SPEC = pl.BlockSpec(memory_space=pltpu.VMEM)
SMEM_SPEC = pl.BlockSpec(memory_space=pltpu.SMEM)


def move(piece, perm, axis="corpus"):
    return lax.ppermute(piece, axis, perm)


def with_core(pieces):
    return [p for piece in pieces for p in (piece, move(piece, CORE))]


def first_stage(own):
    return [own, move(own, CROSS), move(own, AHEAD), move(own, BACK)]


def second_stage(own, cross, behind, ahead):
    return [move(cross, AHEAD), move(behind, AHEAD), move(ahead, CROSS)]


def third_stage(cross_behind, far, cross_ahead):
    return [move(cross_behind, AHEAD)]


def places():
    place = lax.axis_index("corpus")
    z, x, core = place // (NX * NC), place // NC % NX, place % NC
    chips, cores = [], []
    for dz, dx in ROLES:
        for c in (core, 1 - core):
            chips.append(((z + dz * (1 - 2 * c) + NZ) % NZ) * NX + (x + dx) % NX)
            cores.append(c)
    return jnp.stack(chips), jnp.stack(cores)


def blocks_kernel(weights, out, sems):
    wide = out.shape[2]
    copies = [
        pltpu.make_async_copy(weights.at[0, :, pl.ds(i * wide, wide)], out.at[i], sems.at[i])
        for i in range(out.shape[0])
    ]
    for copy in copies:
        copy.start()
    for copy in copies:
        copy.wait()


def column_blocks(weights, count):
    _, rows, columns = weights.shape
    return pl.pallas_call(
        blocks_kernel,
        out_shape=jax.ShapeDtypeStruct((count, rows, columns // count), weights.dtype),
        in_specs=[HBM_SPEC],
        out_specs=VMEM_SPEC,
        scratch_shapes=[pltpu.SemaphoreType.DMA((count,))],
    )(weights)


def condition_kernel(n, place, *refs):
    pieces, weights, (out, held, rows, sems) = refs[:n], refs[n], refs[n + 1 :]
    tall = pieces[0].shape[0]
    loads = [pltpu.make_async_copy(weights, held, sems.at[n])]
    for i, piece in enumerate(pieces):
        loads.append(pltpu.make_async_copy(piece, rows.at[pl.ds(i * tall, tall), :], sems.at[i]))
    for load in loads:
        load.start()
    for load in loads:
        load.wait()
    done = jnp.dot(rows[...], held[...], preferred_element_type=jnp.float32).astype(jnp.bfloat16)
    to_places(place, n, tall, done, out)


def to_places(place, n, tall, done, out):
    few = tall // CHUNKS
    for i in range(n):
        for k in range(CHUNKS):
            to = pl.multiple_of(place[k, i] * few, few)
            out[pl.ds(to, few), :] = done[i * tall + k * few : i * tall + (k + 1) * few, :]


def condition(place, pieces, weights):
    tall, depth = pieces[0].shape
    wide = weights.shape[1]
    n = len(pieces)
    return pl.pallas_call(
        functools.partial(condition_kernel, n),
        out_shape=[
            jax.ShapeDtypeStruct((CHIPS * NC * tall, wide), jnp.bfloat16),
            jax.ShapeDtypeStruct(weights.shape, weights.dtype),
        ],
        in_specs=[SMEM_SPEC] + [ANY_SPEC] * n + [HBM_SPEC],
        out_specs=[VMEM_SPEC] * 2,
        scratch_shapes=[pltpu.VMEM((n * tall, depth), jnp.bfloat16), pltpu.SemaphoreType.DMA((n + 1,))],
        compiler_params=pltpu.CompilerParams(vmem_limit_bytes=48 * 2**20),
        cost_estimate=pl.CostEstimate(
            flops=2 * n * tall * depth * wide, bytes_accessed=(n * tall + wide) * depth * 2, transcendentals=0
        ),
    )(place, *pieces, weights)


def condition_rest_kernel(n, place, *refs):
    pieces, (weights, into, out) = refs[:n], refs[n:]
    tall = pieces[0].shape[0]
    rows = jnp.concatenate([piece[...] for piece in pieces], axis=0)
    done = jnp.dot(rows, weights[...], preferred_element_type=jnp.float32).astype(jnp.bfloat16)
    out[...] = into[...]
    to_places(place, n, tall, done, out)


def condition_rest(place, pieces, weights, into):
    tall, depth = pieces[0].shape
    n = len(pieces)
    return pl.pallas_call(
        functools.partial(condition_rest_kernel, n),
        out_shape=jax.ShapeDtypeStruct(into.shape, into.dtype),
        in_specs=[SMEM_SPEC] + [VMEM_SPEC] * (n + 2),
        out_specs=VMEM_SPEC,
        compiler_params=pltpu.CompilerParams(vmem_limit_bytes=SCOPED),
        cost_estimate=pl.CostEstimate(
            flops=2 * n * tall * depth * into.shape[1], bytes_accessed=2**22, transcendentals=0
        ),
    )(place, *pieces, weights, into)


def score_kernel(n, adds, last, blocks, *refs):
    pieces, docs = refs[:n], refs[n]
    wide = pieces[0].shape[1]
    if last:
        outs = refs[n + 1 + adds :]
        rows = jnp.concatenate([piece[...] for piece in pieces], axis=1)
    else:
        outs, (packed, sems) = refs[n + 1 + adds : -2], refs[-2:]
        copies = [
            pltpu.make_async_copy(piece, packed.at[:, pl.ds(i * wide, wide)], sems.at[i])
            for i, piece in enumerate(pieces)
        ]
        for copy in copies:
            copy.start()
        for copy in copies:
            copy.wait()
        rows = packed[...]
    for j in range(docs.shape[0] // STEP):
        at = slice(j * STEP, (j + 1) * STEP)
        held = jnp.concatenate(
            [docs[at, pl.ds(pl.multiple_of(blocks[i] * wide, wide), wide)] for i in range(n)], axis=1
        )
        part = lax.dot_general(rows, held, (((1,), (1,)), ((), ())), preferred_element_type=jnp.float32)
        if adds:
            part += refs[n + 1][:, at]
        start = 0
        for out in outs:
            out[:, at] = part[start : start + out.shape[0], :].astype(out.dtype)
            start += out.shape[0]


def score(blocks, pieces, docs, before=None, last=False):
    rows, wide = pieces[0].shape
    n_docs = docs.shape[0]
    n = len(pieces)
    given = [] if before is None else [before]
    if last:
        tall = rows // CHUNKS
        shapes = [
            jax.ShapeDtypeStruct((tall // count, n_docs), jnp.bfloat16 if i else jnp.float32)
            for count in (NH, NY)
            for i in range(count)
        ]
    else:
        shapes = [jax.ShapeDtypeStruct((rows, n_docs), jnp.float32)]
    return pl.pallas_call(
        functools.partial(score_kernel, n, len(given), last),
        out_shape=shapes,
        in_specs=[SMEM_SPEC] + [VMEM_SPEC if last else ANY_SPEC] * n + [VMEM_SPEC] * (1 + len(given)),
        out_specs=[VMEM_SPEC] * len(shapes),
        scratch_shapes=[] if last else [pltpu.VMEM((rows, n * wide), jnp.bfloat16), pltpu.SemaphoreType.DMA((n,))],
        input_output_aliases={n + 2: 0} if given and not last else {},
        compiler_params=pltpu.CompilerParams(vmem_limit_bytes=SCOPED),
        cost_estimate=pl.CostEstimate(
            flops=2 * rows * n_docs * n * wide, bytes_accessed=(rows + n_docs) * n * wide * 2, transcendentals=0
        ),
    )(blocks, *pieces, docs, *given)


def exchange_y(own, ahead, far, back):
    steps = ((ahead, 1), (back, -1), (far, 2))
    return [own] + [move(part, group_perm(0, dy), "group") for part, dy in steps]


def exchange_h(own, other):
    return [own, move(other, group_perm(1, 0), "group")]


def added(parts):
    return sum(part.astype(jnp.float32) for part in parts)


def parts_of(rows, count):
    tall = rows.shape[0] // count
    return [rows[i * tall : (i + 1) * tall].astype(jnp.bfloat16 if i else jnp.float32) for i in range(count)]


def local(queries, precond, documents):
    rows, feat = queries.shape
    h, y = lax.axis_index("group") // NY, lax.axis_index("group") % NY
    chips, cores = places()
    dy, dh = (chips % NY - y + NY) % NY, (chips // NY - h + NH) % NH
    place = jnp.stack([(dh * NY + dy) * NC + cores, GROUP * NC + (dy * NH + dh) * NC + cores])
    blocks = chips * NC + cores
    early = NC * STAGES[1][1]
    half = NC * STAGES[0][1]

    one = lax.optimization_barrier(first_stage(queries))
    weights = lax.all_to_all(column_blocks(precond, CHIPS * NC), "corpus", 0, 0, tiled=True).reshape(feat, -1)
    two = second_stage(*one)
    three = third_stage(*two)
    conditioned, weights = condition(place[:, :early], with_core(one + two), weights)
    three, conditioned = lax.optimization_barrier((three, conditioned))
    conditioned = condition_rest(place[:, early:], with_core(three), weights, conditioned)

    one = first_stage(conditioned)
    two = second_stage(*one)
    (scores,) = score(blocks[:half], with_core(one), documents)
    two, scores = lax.optimization_barrier((two, scores))
    three = third_stage(*two)
    (scores,) = score(blocks[half:early], with_core(two), documents, scores)
    three, scores = lax.optimization_barrier((three, scores))
    parts = score(blocks[early:], with_core(three), documents, scores, last=True)
    first, second = lax.optimization_barrier((exchange_h(*parts[:NH]), exchange_y(*parts[NH:])))
    first = added(exchange_y(*parts_of(added(first), NY)))
    second = added(exchange_h(*parts_of(added(second), NH)))
    totals = [total.reshape(NC, rows // CHUNKS, -1) for total in (first, second)]
    scores = jnp.concatenate(totals, axis=1).reshape(NC * rows, -1)
    return scores / jnp.sqrt(jnp.float32(GROUP * feat))


def solution(mesh):
    placed = (P("corpus", "group"), P("group", "corpus", None), P("corpus", "group"))
    return jax.shard_map(
        local, mesh=mesh, in_specs=placed, out_specs=P("group", "corpus"), check_vma=False
    )
```

```python
import functools

import jax
import jax.numpy as jnp
from jax import lax
from jax.experimental import pallas as pl
from jax.experimental.pallas import tpu as pltpu
from jax.sharding import PartitionSpec as P

NZ, NX, NC, NH, NY = 4, 2, 2, 2, 4
CHIPS = NZ * NX
GROUP = NH * NY
ROLES = ((0, 0), (0, 1), (-1, 0), (1, 0), (-1, 1), (2, 0), (1, 1), (2, 1))
STAGES = ((0, 4), (4, 7), (7, 8))


def corpus_perm(move):
    pairs = []
    for z in range(NZ):
        for x in range(NX):
            for c in range(NC):
                dz, dx, dc = move(1 - 2 * c)
                to = ((z + dz) % NZ, (x + dx) % NX, (c + dc) % NC)
                pairs.append(((z * NX + x) * NC + c, (to[0] * NX + to[1]) * NC + to[2]))
    return pairs


def group_perm(dh, dy):
    return [(h * NY + y, (h + dh) % NH * NY + (y + dy) % NY) for h in range(NH) for y in range(NY)]


AHEAD = corpus_perm(lambda d: (d, 0, 0))
BACK = corpus_perm(lambda d: (-d, 0, 0))
CROSS = corpus_perm(lambda d: (0, 1, 0))
CORE = corpus_perm(lambda d: (0, 0, 1))


CHUNKS = 2
STEP = 512
SCOPED = 12 * 2**20
ANY_SPEC = pl.BlockSpec(memory_space=pl.ANY)
HBM_SPEC = pl.BlockSpec(memory_space=pltpu.HBM)
VMEM_SPEC = pl.BlockSpec(memory_space=pltpu.VMEM)
SMEM_SPEC = pl.BlockSpec(memory_space=pltpu.SMEM)


def move(piece, perm, axis="corpus"):
    return lax.ppermute(piece, axis, perm)


def with_core(pieces):
    return [p for piece in pieces for p in (piece, move(piece, CORE))]


def first_stage(own):
    return [own, move(own, CROSS), move(own, AHEAD), move(own, BACK)]


def second_stage(own, cross, behind, ahead):
    return [move(cross, AHEAD), move(behind, AHEAD), move(ahead, CROSS)]


def third_stage(cross_behind, far, cross_ahead):
    return [move(cross_behind, AHEAD)]


def places():
    place = lax.axis_index("corpus")
    z, x, core = place // (NX * NC), place // NC % NX, place % NC
    chips, cores = [], []
    for dz, dx in ROLES:
        for c in (core, 1 - core):
            chips.append(((z + dz * (1 - 2 * c) + NZ) % NZ) * NX + (x + dx) % NX)
            cores.append(c)
    return jnp.stack(chips), jnp.stack(cores)


def blocks_kernel(weights, out, sems):
    wide = out.shape[2]
    copies = [
        pltpu.make_async_copy(weights.at[0, :, pl.ds(i * wide, wide)], out.at[i], sems.at[i])
        for i in range(out.shape[0])
    ]
    for copy in copies:
        copy.start()
    for copy in copies:
        copy.wait()


def column_blocks(weights, count):
    _, rows, columns = weights.shape
    return pl.pallas_call(
        blocks_kernel,
        out_shape=jax.ShapeDtypeStruct((count, rows, columns // count), weights.dtype),
        in_specs=[HBM_SPEC],
        out_specs=VMEM_SPEC,
        scratch_shapes=[pltpu.SemaphoreType.DMA((count,))],
    )(weights)


def condition_kernel(n, place, *refs):
    pieces, weights, (out, held, rows, sems) = refs[:n], refs[n], refs[n + 1 :]
    tall = pieces[0].shape[0]
    loads = [pltpu.make_async_copy(weights, held, sems.at[n])]
    for i, piece in enumerate(pieces):
        loads.append(pltpu.make_async_copy(piece, rows.at[pl.ds(i * tall, tall), :], sems.at[i]))
    for load in loads:
        load.start()
    for load in loads:
        load.wait()
    done = jnp.dot(rows[...], held[...], preferred_element_type=jnp.float32).astype(jnp.bfloat16)
    to_places(place, n, tall, done, out)


def to_places(place, n, tall, done, out):
    few = tall // CHUNKS
    for i in range(n):
        for k in range(CHUNKS):
            to = pl.multiple_of(place[k, i] * few, few)
            out[pl.ds(to, few), :] = done[i * tall + k * few : i * tall + (k + 1) * few, :]


def condition(place, pieces, weights):
    tall, depth = pieces[0].shape
    wide = weights.shape[1]
    n = len(pieces)
    return pl.pallas_call(
        functools.partial(condition_kernel, n),
        out_shape=[
            jax.ShapeDtypeStruct((CHIPS * NC * tall, wide), jnp.bfloat16),
            jax.ShapeDtypeStruct(weights.shape, weights.dtype),
        ],
        in_specs=[SMEM_SPEC] + [ANY_SPEC] * n + [HBM_SPEC],
        out_specs=[VMEM_SPEC] * 2,
        scratch_shapes=[pltpu.VMEM((n * tall, depth), jnp.bfloat16), pltpu.SemaphoreType.DMA((n + 1,))],
        compiler_params=pltpu.CompilerParams(vmem_limit_bytes=52 * 2**20),
        cost_estimate=pl.CostEstimate(
            flops=2 * n * tall * depth * wide, bytes_accessed=(n * tall + wide) * depth * 2, transcendentals=0
        ),
    )(place, *pieces, weights)


def condition_rest_kernel(n, place, *refs):
    pieces, (weights, into, out) = refs[:n], refs[n:]
    tall = pieces[0].shape[0]
    rows = jnp.concatenate([piece[...] for piece in pieces], axis=0)
    done = jnp.dot(rows, weights[...], preferred_element_type=jnp.float32).astype(jnp.bfloat16)
    out[...] = into[...]
    to_places(place, n, tall, done, out)


def condition_rest(place, pieces, weights, into):
    tall, depth = pieces[0].shape
    n = len(pieces)
    return pl.pallas_call(
        functools.partial(condition_rest_kernel, n),
        out_shape=jax.ShapeDtypeStruct(into.shape, into.dtype),
        in_specs=[SMEM_SPEC] + [VMEM_SPEC] * (n + 2),
        out_specs=VMEM_SPEC,
        compiler_params=pltpu.CompilerParams(vmem_limit_bytes=24 * 2**20),
        cost_estimate=pl.CostEstimate(
            flops=2 * n * tall * depth * into.shape[1], bytes_accessed=2**22, transcendentals=0
        ),
    )(place, *pieces, weights, into)


def packed_rows(pieces, packed, sems):
    wide = pieces[0].shape[1]
    copies = [
        pltpu.make_async_copy(piece, packed.at[:, pl.ds(i * wide, wide)], sems.at[i])
        for i, piece in enumerate(pieces)
    ]
    for copy in copies:
        copy.start()
    for copy in copies:
        copy.wait()
    return packed[...]


def product(rows, columns):
    return lax.dot_general(rows, columns, (((1,), (1,)), ((), ())), preferred_element_type=jnp.float32)


def score_first_kernel(n, blocks, *refs):
    pieces, (docs, out, rest, packed, sems) = refs[:n], refs[n:]
    wide = pieces[0].shape[1]
    rows = packed_rows(pieces, packed, sems)
    for j in range(docs.shape[0] // STEP):
        at = slice(j * STEP, (j + 1) * STEP)
        columns = [
            docs[at, pl.ds(pl.multiple_of(blocks[i] * wide, wide), wide)] for i in range(docs.shape[1] // wide)
        ]
        out[:, at] = product(rows, jnp.concatenate(columns[:n], axis=1))
        rest[at, :] = jnp.concatenate(columns[n:], axis=1)


def score_first(blocks, pieces, docs):
    rows, wide = pieces[0].shape
    n_docs, depth = docs.shape
    n = len(pieces)
    return pl.pallas_call(
        functools.partial(score_first_kernel, n),
        out_shape=[
            jax.ShapeDtypeStruct((rows, n_docs), jnp.float32),
            jax.ShapeDtypeStruct((n_docs, depth - n * wide), docs.dtype),
        ],
        in_specs=[SMEM_SPEC] + [ANY_SPEC] * n + [VMEM_SPEC],
        out_specs=[VMEM_SPEC] * 2,
        scratch_shapes=[pltpu.VMEM((rows, n * wide), jnp.bfloat16), pltpu.SemaphoreType.DMA((n,))],
        compiler_params=pltpu.CompilerParams(vmem_limit_bytes=SCOPED),
        cost_estimate=pl.CostEstimate(
            flops=2 * rows * n_docs * n * wide, bytes_accessed=(rows + n_docs) * n * wide * 2, transcendentals=0
        ),
    )(blocks, *pieces, docs)


def score_next_kernel(n, start, *refs):
    pieces, (columns, before, out, packed, sems) = refs[:n], refs[n:]
    rows = packed_rows(pieces, packed, sems)
    for j in range(columns.shape[0] // STEP):
        at = slice(j * STEP, (j + 1) * STEP)
        out[:, at] = before[:, at] + product(rows, columns[at, start : start + rows.shape[1]])


def score_next(start, pieces, columns, before):
    rows, wide = pieces[0].shape
    n_docs = columns.shape[0]
    n = len(pieces)
    return pl.pallas_call(
        functools.partial(score_next_kernel, n, start),
        out_shape=jax.ShapeDtypeStruct((rows, n_docs), jnp.float32),
        in_specs=[ANY_SPEC] * n + [VMEM_SPEC] * 2,
        out_specs=VMEM_SPEC,
        scratch_shapes=[pltpu.VMEM((rows, n * wide), jnp.bfloat16), pltpu.SemaphoreType.DMA((n,))],
        input_output_aliases={n + 1: 0},
        compiler_params=pltpu.CompilerParams(vmem_limit_bytes=SCOPED),
        cost_estimate=pl.CostEstimate(
            flops=2 * rows * n_docs * n * wide, bytes_accessed=(rows + n_docs) * n * wide * 2, transcendentals=0
        ),
    )(*pieces, columns, before)


def score_last_kernel(n, start, *refs):
    pieces, columns, before, outs = refs[:n], refs[n], refs[n + 1], refs[n + 2 :]
    rows = jnp.concatenate([piece[...] for piece in pieces], axis=1)
    for j in range(columns.shape[0] // STEP):
        at = slice(j * STEP, (j + 1) * STEP)
        part = before[:, at] + product(rows, columns[at, start:])
        top = 0
        for out in outs:
            out[:, at] = part[top : top + out.shape[0], :].astype(out.dtype)
            top += out.shape[0]


def score_last(start, pieces, columns, before):
    rows, wide = pieces[0].shape
    n_docs = columns.shape[0]
    n = len(pieces)
    shapes = [
        jax.ShapeDtypeStruct((rows // CHUNKS // count, n_docs), jnp.bfloat16 if i else jnp.float32)
        for count in (NH, NY)
        for i in range(count)
    ]
    return pl.pallas_call(
        functools.partial(score_last_kernel, n, start),
        out_shape=shapes,
        in_specs=[VMEM_SPEC] * (n + 2),
        out_specs=[VMEM_SPEC] * len(shapes),
        compiler_params=pltpu.CompilerParams(vmem_limit_bytes=SCOPED),
        cost_estimate=pl.CostEstimate(
            flops=2 * rows * n_docs * n * wide, bytes_accessed=2**24, transcendentals=0
        ),
    )(*pieces, columns, before)


def exchange_y(own, ahead, far, back):
    steps = ((ahead, 1), (back, -1), (far, 2))
    return [own] + [move(part, group_perm(0, dy), "group") for part, dy in steps]


def exchange_h(own, other):
    return [own, move(other, group_perm(1, 0), "group")]


def added(parts):
    return sum(part.astype(jnp.float32) for part in parts)


def parts_of(rows, count):
    tall = rows.shape[0] // count
    return [rows[i * tall : (i + 1) * tall].astype(jnp.bfloat16 if i else jnp.float32) for i in range(count)]


def local(queries, precond, documents):
    rows, feat = queries.shape
    h, y = lax.axis_index("group") // NY, lax.axis_index("group") % NY
    chips, cores = places()
    dy, dh = (chips % NY - y + NY) % NY, (chips // NY - h + NH) % NH
    place = jnp.stack([(dh * NY + dy) * NC + cores, GROUP * NC + (dy * NH + dh) * NC + cores])
    blocks = chips * NC + cores
    early = NC * STAGES[1][1]
    half = NC * STAGES[0][1]

    one = lax.optimization_barrier(first_stage(queries))
    weights = lax.all_to_all(column_blocks(precond, CHIPS * NC), "corpus", 0, 0, tiled=True).reshape(feat, -1)
    two = second_stage(*one)
    three = third_stage(*two)
    conditioned, weights = condition(place[:, :early], with_core(one + two), weights)
    three, conditioned = lax.optimization_barrier((three, conditioned))
    conditioned = condition_rest(place[:, early:], with_core(three), weights, conditioned)

    wide = conditioned.shape[1]
    one = first_stage(conditioned)
    scores, columns = score_first(blocks, with_core(one[:1]), documents)
    one, scores = lax.optimization_barrier((one, scores))
    two = second_stage(*one)
    scores = score_next(0, with_core(one[1:]), columns, scores)
    two[0], scores = lax.optimization_barrier((two[0], scores))
    three = third_stage(*two)
    scores, *_ = lax.optimization_barrier((scores, three[0]))
    scores = score_next((half - NC) * wide, with_core(two), columns, scores)
    parts = score_last((early - NC) * wide, with_core(three), columns, scores)
    first, second = exchange_h(*parts[:NH]), exchange_y(*parts[NH:])
    second, first = lax.optimization_barrier((second, first))
    first = parts_of(added(first), NY)
    first = added(exchange_y(*first))
    second = added(exchange_h(*parts_of(added(second), NH)))
    totals = [total.reshape(NC, rows // CHUNKS, -1) for total in (first, second)]
    scores = jnp.concatenate(totals, axis=1).reshape(NC * rows, -1)
    return scores / jnp.sqrt(jnp.float32(GROUP * feat))


def solution(mesh):
    placed = (P("corpus", "group"), P("group", "corpus", None), P("corpus", "group"))
    return jax.shard_map(
        local, mesh=mesh, in_specs=placed, out_specs=P("group", "corpus"), check_vma=False
    )
```

```python
import functools

import jax
import jax.numpy as jnp
from jax import lax
from jax.experimental import pallas as pl
from jax.experimental.pallas import tpu as pltpu
from jax.sharding import PartitionSpec as P

NZ, NX, NC, NH, NY = 4, 2, 2, 2, 4
CHIPS = NZ * NX
GROUP = NH * NY
ROLES = ((0, 0), (0, 1), (-1, 0), (1, 0), (-1, 1), (2, 0), (1, 1), (2, 1))
STAGES = ((0, 4), (4, 7), (7, 8))


def corpus_perm(move):
    pairs = []
    for z in range(NZ):
        for x in range(NX):
            for c in range(NC):
                dz, dx, dc = move(1 - 2 * c)
                to = ((z + dz) % NZ, (x + dx) % NX, (c + dc) % NC)
                pairs.append(((z * NX + x) * NC + c, (to[0] * NX + to[1]) * NC + to[2]))
    return pairs


def group_perm(dh, dy):
    return [(h * NY + y, (h + dh) % NH * NY + (y + dy) % NY) for h in range(NH) for y in range(NY)]


AHEAD = corpus_perm(lambda d: (d, 0, 0))
BACK = corpus_perm(lambda d: (-d, 0, 0))
CROSS = corpus_perm(lambda d: (0, 1, 0))
CORE = corpus_perm(lambda d: (0, 0, 1))


CHUNKS = 2
STEP = 512
SCOPED = 12 * 2**20
ANY_SPEC = pl.BlockSpec(memory_space=pl.ANY)
HBM_SPEC = pl.BlockSpec(memory_space=pltpu.HBM)
VMEM_SPEC = pl.BlockSpec(memory_space=pltpu.VMEM)
SMEM_SPEC = pl.BlockSpec(memory_space=pltpu.SMEM)


def move(piece, perm, axis="corpus"):
    return lax.ppermute(piece, axis, perm)


def with_core(pieces):
    return [p for piece in pieces for p in (piece, move(piece, CORE))]


def first_stage(own):
    return [own, move(own, CROSS), move(own, AHEAD), move(own, BACK)]


def second_stage(own, cross, behind, ahead):
    return [move(cross, AHEAD), move(behind, AHEAD), move(ahead, CROSS)]


def third_stage(cross_behind, far, cross_ahead):
    return [move(cross_behind, AHEAD)]


def places():
    place = lax.axis_index("corpus")
    z, x, core = place // (NX * NC), place // NC % NX, place % NC
    chips, cores = [], []
    for dz, dx in ROLES:
        for c in (core, 1 - core):
            chips.append(((z + dz * (1 - 2 * c) + NZ) % NZ) * NX + (x + dx) % NX)
            cores.append(c)
    return jnp.stack(chips), jnp.stack(cores)


def blocks_kernel(weights, out, sems):
    wide = out.shape[2]
    copies = [
        pltpu.make_async_copy(weights.at[0, :, pl.ds(i * wide, wide)], out.at[i], sems.at[i])
        for i in range(out.shape[0])
    ]
    for copy in copies:
        copy.start()
    for copy in copies:
        copy.wait()


def column_blocks(weights, count):
    _, rows, columns = weights.shape
    return pl.pallas_call(
        blocks_kernel,
        out_shape=jax.ShapeDtypeStruct((count, rows, columns // count), weights.dtype),
        in_specs=[HBM_SPEC],
        out_specs=VMEM_SPEC,
        scratch_shapes=[pltpu.SemaphoreType.DMA((count,))],
    )(weights)


def condition_kernel(n, place, *refs):
    pieces, weights, (out, held, rows, sems) = refs[:n], refs[n], refs[n + 1 :]
    tall = pieces[0].shape[0]
    loads = [pltpu.make_async_copy(weights, held, sems.at[n])]
    for i, piece in enumerate(pieces):
        loads.append(pltpu.make_async_copy(piece, rows.at[pl.ds(i * tall, tall), :], sems.at[i]))
    for load in loads:
        load.start()
    for load in loads:
        load.wait()
    done = jnp.dot(rows[...], held[...], preferred_element_type=jnp.float32).astype(jnp.bfloat16)
    to_places(place, n, tall, done, out)


def to_places(place, n, tall, done, out):
    few = tall // CHUNKS
    for i in range(n):
        for k in range(CHUNKS):
            to = pl.multiple_of(place[k, i] * few, few)
            out[pl.ds(to, few), :] = done[i * tall + k * few : i * tall + (k + 1) * few, :]


def condition(place, pieces, weights):
    tall, depth = pieces[0].shape
    wide = weights.shape[1]
    n = len(pieces)
    return pl.pallas_call(
        functools.partial(condition_kernel, n),
        out_shape=[
            jax.ShapeDtypeStruct((CHIPS * NC * tall, wide), jnp.bfloat16),
            jax.ShapeDtypeStruct(weights.shape, weights.dtype),
        ],
        in_specs=[SMEM_SPEC] + [ANY_SPEC] * n + [HBM_SPEC],
        out_specs=[VMEM_SPEC] * 2,
        scratch_shapes=[pltpu.VMEM((n * tall, depth), jnp.bfloat16), pltpu.SemaphoreType.DMA((n + 1,))],
        compiler_params=pltpu.CompilerParams(vmem_limit_bytes=52 * 2**20),
        cost_estimate=pl.CostEstimate(
            flops=2 * n * tall * depth * wide, bytes_accessed=(n * tall + wide) * depth * 2, transcendentals=0
        ),
    )(place, *pieces, weights)


def condition_rest_kernel(n, place, *refs):
    pieces, (weights, into, out) = refs[:n], refs[n:]
    tall = pieces[0].shape[0]
    rows = jnp.concatenate([piece[...] for piece in pieces], axis=0)
    done = jnp.dot(rows, weights[...], preferred_element_type=jnp.float32).astype(jnp.bfloat16)
    out[...] = into[...]
    to_places(place, n, tall, done, out)


def condition_rest(place, pieces, weights, into):
    tall, depth = pieces[0].shape
    n = len(pieces)
    return pl.pallas_call(
        functools.partial(condition_rest_kernel, n),
        out_shape=jax.ShapeDtypeStruct(into.shape, into.dtype),
        in_specs=[SMEM_SPEC] + [VMEM_SPEC] * (n + 2),
        out_specs=VMEM_SPEC,
        compiler_params=pltpu.CompilerParams(vmem_limit_bytes=24 * 2**20),
        cost_estimate=pl.CostEstimate(
            flops=2 * n * tall * depth * into.shape[1], bytes_accessed=2**22, transcendentals=0
        ),
    )(place, *pieces, weights, into)


def packed_rows(pieces, packed, sems):
    wide = pieces[0].shape[1]
    copies = [
        pltpu.make_async_copy(piece, packed.at[:, pl.ds(i * wide, wide)], sems.at[i])
        for i, piece in enumerate(pieces)
    ]
    for copy in copies:
        copy.start()
    for copy in copies:
        copy.wait()
    return packed[...]


def product(rows, columns):
    return lax.dot_general(rows, columns, (((1,), (1,)), ((), ())), preferred_element_type=jnp.float32)


def score_first_kernel(n, blocks, *refs):
    pieces, (docs, out, rest, packed, sems) = refs[:n], refs[n:]
    wide = pieces[0].shape[1]
    rows = packed_rows(pieces, packed, sems)
    for j in range(docs.shape[0] // STEP):
        at = slice(j * STEP, (j + 1) * STEP)
        columns = [
            docs[at, pl.ds(pl.multiple_of(blocks[i] * wide, wide), wide)] for i in range(docs.shape[1] // wide)
        ]
        out[:, at] = product(rows, jnp.concatenate(columns[:n], axis=1))
        rest[at, :] = jnp.concatenate(columns[n:], axis=1)


def score_first(blocks, pieces, docs):
    rows, wide = pieces[0].shape
    n_docs, depth = docs.shape
    n = len(pieces)
    return pl.pallas_call(
        functools.partial(score_first_kernel, n),
        out_shape=[
            jax.ShapeDtypeStruct((rows, n_docs), jnp.float32),
            jax.ShapeDtypeStruct((n_docs, depth - n * wide), docs.dtype),
        ],
        in_specs=[SMEM_SPEC] + [ANY_SPEC] * n + [VMEM_SPEC],
        out_specs=[VMEM_SPEC] * 2,
        scratch_shapes=[pltpu.VMEM((rows, n * wide), jnp.bfloat16), pltpu.SemaphoreType.DMA((n,))],
        compiler_params=pltpu.CompilerParams(vmem_limit_bytes=SCOPED),
        cost_estimate=pl.CostEstimate(
            flops=2 * rows * n_docs * n * wide, bytes_accessed=(rows + n_docs) * n * wide * 2, transcendentals=0
        ),
    )(blocks, *pieces, docs)


def score_next_kernel(n, start, *refs):
    pieces, (columns, before, out, packed, sems) = refs[:n], refs[n:]
    rows = packed_rows(pieces, packed, sems)
    for j in range(columns.shape[0] // STEP):
        at = slice(j * STEP, (j + 1) * STEP)
        out[:, at] = before[:, at] + product(rows, columns[at, start : start + rows.shape[1]])


def score_next(start, pieces, columns, before):
    rows, wide = pieces[0].shape
    n_docs = columns.shape[0]
    n = len(pieces)
    return pl.pallas_call(
        functools.partial(score_next_kernel, n, start),
        out_shape=jax.ShapeDtypeStruct((rows, n_docs), jnp.float32),
        in_specs=[ANY_SPEC] * n + [VMEM_SPEC] * 2,
        out_specs=VMEM_SPEC,
        scratch_shapes=[pltpu.VMEM((rows, n * wide), jnp.bfloat16), pltpu.SemaphoreType.DMA((n,))],
        input_output_aliases={n + 1: 0},
        compiler_params=pltpu.CompilerParams(vmem_limit_bytes=SCOPED),
        cost_estimate=pl.CostEstimate(
            flops=2 * rows * n_docs * n * wide, bytes_accessed=(rows + n_docs) * n * wide * 2, transcendentals=0
        ),
    )(*pieces, columns, before)


def score_last_kernel(n, start, chunk, *refs):
    pieces, columns, before, outs = refs[:n], refs[n], refs[n + 1], refs[n + 2 :]
    tall = before.shape[0] // CHUNKS
    mine = slice(chunk * tall, (chunk + 1) * tall)
    rows = jnp.concatenate([piece[mine, :] for piece in pieces], axis=1)
    for j in range(columns.shape[0] // STEP):
        at = slice(j * STEP, (j + 1) * STEP)
        part = before[mine, at] + product(rows, columns[at, start:])
        top = 0
        for out in outs:
            out[:, at] = part[top : top + out.shape[0], :].astype(out.dtype)
            top += out.shape[0]


def score_last(start, pieces, columns, before, chunk, heights):
    rows, wide = pieces[0].shape
    n_docs = columns.shape[0]
    n = len(pieces)
    shapes = [
        jax.ShapeDtypeStruct((tall, n_docs), jnp.bfloat16 if i else jnp.float32) for i, tall in enumerate(heights)
    ]
    return pl.pallas_call(
        functools.partial(score_last_kernel, n, start, chunk),
        out_shape=shapes,
        in_specs=[VMEM_SPEC] * (n + 2),
        out_specs=[VMEM_SPEC] * len(shapes),
        compiler_params=pltpu.CompilerParams(vmem_limit_bytes=SCOPED),
        cost_estimate=pl.CostEstimate(
            flops=2 * rows // CHUNKS * n_docs * n * wide, bytes_accessed=2**23, transcendentals=0
        ),
    )(*pieces, columns, before)


def exchange_y(own, ahead, far, back):
    steps = ((ahead, 1), (back, -1), (far, 2))
    return [own] + [move(part, group_perm(0, dy), "group") for part, dy in steps]


def exchange_h(own, other):
    return [own, move(other, group_perm(1, 0), "group")]


def added(parts):
    return sum(part.astype(jnp.float32) for part in parts)


def parts_of(rows, count):
    tall = rows.shape[0] // count
    return [rows[i * tall : (i + 1) * tall].astype(jnp.bfloat16 if i else jnp.float32) for i in range(count)]


def local(queries, precond, documents):
    rows, feat = queries.shape
    h, y = lax.axis_index("group") // NY, lax.axis_index("group") % NY
    chips, cores = places()
    dy, dh = (chips % NY - y + NY) % NY, (chips // NY - h + NH) % NH
    place = jnp.stack([(dh * NY + dy) * NC + cores, GROUP * NC + (dy * NH + dh) * NC + cores])
    blocks = chips * NC + cores
    early = NC * STAGES[1][1]
    half = NC * STAGES[0][1]

    one = lax.optimization_barrier(first_stage(queries))
    weights = lax.all_to_all(column_blocks(precond, CHIPS * NC), "corpus", 0, 0, tiled=True).reshape(feat, -1)
    two = second_stage(*one)
    three = third_stage(*two)
    conditioned, weights = condition(place[:, :early], with_core(one + two), weights)
    three, conditioned = lax.optimization_barrier((three, conditioned))
    conditioned = condition_rest(place[:, early:], with_core(three), weights, conditioned)

    wide = conditioned.shape[1]
    one = first_stage(conditioned)
    scores, columns = score_first(blocks, with_core(one[:1]), documents)
    one[1:3], scores = lax.optimization_barrier((one[1:3], scores))
    two = second_stage(*one)
    scores = score_next(0, with_core(one[1:]), columns, scores)
    two[0], scores = lax.optimization_barrier((two[0], scores))
    three = third_stage(*two)
    scores, *_ = lax.optimization_barrier((scores, three[0]))
    scores = score_next((half - NC) * wide, with_core(two), columns, scores)
    start, pieces = (early - NC) * wide, with_core(three)
    tall = conditioned.shape[0] // CHUNKS
    first = score_last(start, pieces, columns, scores, 0, [tall // NH] * NH)
    scores, *_ = lax.optimization_barrier((scores, first[0]))
    part, less = tall // NY, tall // GROUP
    own, ahead, far, across, back = score_last(start, pieces, columns, scores, 1, [part, part, less, less, part])
    go = functools.partial(move, axis="group")
    near = [own, go(ahead, group_perm(0, 1)), go(back, group_perm(0, -1))]
    distant = [go(far, group_perm(0, 2)), go(across, group_perm(1, 2))]
    first, near = lax.optimization_barrier((exchange_h(*first), near))
    first = added(exchange_y(*parts_of(added(first), NY)))
    second = added(exchange_h(*parts_of(added(near), NH)) + distant)
    totals = [total.reshape(NC, rows // CHUNKS, -1) for total in (first, second)]
    scores = jnp.concatenate(totals, axis=1).reshape(NC * rows, -1)
    return scores / jnp.sqrt(jnp.float32(GROUP * feat))


def solution(mesh):
    placed = (P("corpus", "group"), P("group", "corpus", None), P("corpus", "group"))
    return jax.shard_map(
        local, mesh=mesh, in_specs=placed, out_specs=P("group", "corpus"), check_vma=False
    )
```

```python
import functools

import jax
import jax.numpy as jnp
from jax import lax
from jax.experimental import pallas as pl
from jax.experimental.pallas import tpu as pltpu
from jax.sharding import PartitionSpec as P

NZ, NX, NC, NH, NY = 4, 2, 2, 2, 4
CHIPS = NZ * NX
GROUP = NH * NY
ROLES = ((0, 0), (0, 1), (-1, 0), (1, 0), (-1, 1), (2, 0), (1, 1), (2, 1))
STAGES = ((0, 4), (4, 7), (7, 8))


def corpus_perm(move):
    pairs = []
    for z in range(NZ):
        for x in range(NX):
            for c in range(NC):
                dz, dx, dc = move(1 - 2 * c)
                to = ((z + dz) % NZ, (x + dx) % NX, (c + dc) % NC)
                pairs.append(((z * NX + x) * NC + c, (to[0] * NX + to[1]) * NC + to[2]))
    return pairs


def group_perm(dh, dy):
    return [(h * NY + y, (h + dh) % NH * NY + (y + dy) % NY) for h in range(NH) for y in range(NY)]


AHEAD = corpus_perm(lambda d: (d, 0, 0))
BACK = corpus_perm(lambda d: (-d, 0, 0))
CROSS = corpus_perm(lambda d: (0, 1, 0))
CORE = corpus_perm(lambda d: (0, 0, 1))


CHUNKS = 2
STEP = 512
SCOPED = 12 * 2**20
ANY_SPEC = pl.BlockSpec(memory_space=pl.ANY)
HBM_SPEC = pl.BlockSpec(memory_space=pltpu.HBM)
VMEM_SPEC = pl.BlockSpec(memory_space=pltpu.VMEM)
SMEM_SPEC = pl.BlockSpec(memory_space=pltpu.SMEM)


def move(piece, perm, axis="corpus"):
    return lax.ppermute(piece, axis, perm)


def with_core(pieces):
    return [p for piece in pieces for p in (piece, move(piece, CORE))]


def first_stage(own):
    return [own, move(own, CROSS), move(own, AHEAD), move(own, BACK)]


def second_stage(own, cross, behind, ahead):
    return [move(cross, AHEAD), move(behind, AHEAD), move(ahead, CROSS)]


def third_stage(cross_behind, far, cross_ahead):
    return [move(cross_behind, AHEAD)]


def places():
    place = lax.axis_index("corpus")
    z, x, core = place // (NX * NC), place // NC % NX, place % NC
    chips, cores = [], []
    for dz, dx in ROLES:
        for c in (core, 1 - core):
            chips.append(((z + dz * (1 - 2 * c) + NZ) % NZ) * NX + (x + dx) % NX)
            cores.append(c)
    return jnp.stack(chips), jnp.stack(cores)


def blocks_kernel(weights, out, sems):
    wide = out.shape[2]
    copies = [
        pltpu.make_async_copy(weights.at[0, :, pl.ds(i * wide, wide)], out.at[i], sems.at[i])
        for i in range(out.shape[0])
    ]
    for copy in copies:
        copy.start()
    for copy in copies:
        copy.wait()


def column_blocks(weights, count):
    _, rows, columns = weights.shape
    return pl.pallas_call(
        blocks_kernel,
        out_shape=jax.ShapeDtypeStruct((count, rows, columns // count), weights.dtype),
        in_specs=[HBM_SPEC],
        out_specs=VMEM_SPEC,
        scratch_shapes=[pltpu.SemaphoreType.DMA((count,))],
    )(weights)


def condition_kernel(n, place, *refs):
    pieces, weights, (out, held, rows, sems) = refs[:n], refs[n], refs[n + 1 :]
    tall = pieces[0].shape[0]
    loads = [pltpu.make_async_copy(weights, held, sems.at[n])]
    for i, piece in enumerate(pieces):
        loads.append(pltpu.make_async_copy(piece, rows.at[pl.ds(i * tall, tall), :], sems.at[i]))
    for load in loads:
        load.start()
    for load in loads:
        load.wait()
    done = jnp.dot(rows[...], held[...], preferred_element_type=jnp.float32).astype(jnp.bfloat16)
    to_places(place, n, tall, done, out)


def to_places(place, n, tall, done, out):
    few = tall // CHUNKS
    for i in range(n):
        for k in range(CHUNKS):
            to = pl.multiple_of(place[k, i] * few, few)
            out[pl.ds(to, few), :] = done[i * tall + k * few : i * tall + (k + 1) * few, :]


def condition(place, pieces, weights):
    tall, depth = pieces[0].shape
    wide = weights.shape[1]
    n = len(pieces)
    return pl.pallas_call(
        functools.partial(condition_kernel, n),
        out_shape=[
            jax.ShapeDtypeStruct((CHIPS * NC * tall, wide), jnp.bfloat16),
            jax.ShapeDtypeStruct(weights.shape, weights.dtype),
        ],
        in_specs=[SMEM_SPEC] + [ANY_SPEC] * n + [HBM_SPEC],
        out_specs=[VMEM_SPEC] * 2,
        scratch_shapes=[pltpu.VMEM((n * tall, depth), jnp.bfloat16), pltpu.SemaphoreType.DMA((n + 1,))],
        compiler_params=pltpu.CompilerParams(vmem_limit_bytes=52 * 2**20),
        cost_estimate=pl.CostEstimate(
            flops=2 * n * tall * depth * wide, bytes_accessed=(n * tall + wide) * depth * 2, transcendentals=0
        ),
    )(place, *pieces, weights)


def condition_rest_kernel(n, place, *refs):
    pieces, (weights, into, out) = refs[:n], refs[n:]
    tall = pieces[0].shape[0]
    rows = jnp.concatenate([piece[...] for piece in pieces], axis=0)
    done = jnp.dot(rows, weights[...], preferred_element_type=jnp.float32).astype(jnp.bfloat16)
    out[...] = into[...]
    to_places(place, n, tall, done, out)


def condition_rest(place, pieces, weights, into):
    tall, depth = pieces[0].shape
    n = len(pieces)
    return pl.pallas_call(
        functools.partial(condition_rest_kernel, n),
        out_shape=jax.ShapeDtypeStruct(into.shape, into.dtype),
        in_specs=[SMEM_SPEC] + [VMEM_SPEC] * (n + 2),
        out_specs=VMEM_SPEC,
        compiler_params=pltpu.CompilerParams(vmem_limit_bytes=24 * 2**20),
        cost_estimate=pl.CostEstimate(
            flops=2 * n * tall * depth * into.shape[1], bytes_accessed=2**22, transcendentals=0
        ),
    )(place, *pieces, weights, into)


def packed_rows(pieces, packed, sems):
    wide = pieces[0].shape[1]
    copies = [
        pltpu.make_async_copy(piece, packed.at[:, pl.ds(i * wide, wide)], sems.at[i])
        for i, piece in enumerate(pieces)
    ]
    for copy in copies:
        copy.start()
    for copy in copies:
        copy.wait()
    return packed[...]


def product(rows, columns):
    return lax.dot_general(rows, columns, (((1,), (1,)), ((), ())), preferred_element_type=jnp.float32)


def score_first_kernel(n, blocks, *refs):
    pieces, (docs, out, rest, packed, sems) = refs[:n], refs[n:]
    wide = pieces[0].shape[1]
    rows = packed_rows(pieces, packed, sems)
    for j in range(docs.shape[0] // STEP):
        at = slice(j * STEP, (j + 1) * STEP)
        columns = [
            docs[at, pl.ds(pl.multiple_of(blocks[i] * wide, wide), wide)] for i in range(docs.shape[1] // wide)
        ]
        out[:, at] = product(rows, jnp.concatenate(columns[:n], axis=1))
        rest[at, :] = jnp.concatenate(columns[n:], axis=1)


def score_first(blocks, pieces, docs):
    rows, wide = pieces[0].shape
    n_docs, depth = docs.shape
    n = len(pieces)
    return pl.pallas_call(
        functools.partial(score_first_kernel, n),
        out_shape=[
            jax.ShapeDtypeStruct((rows, n_docs), jnp.float32),
            jax.ShapeDtypeStruct((n_docs, depth - n * wide), docs.dtype),
        ],
        in_specs=[SMEM_SPEC] + [ANY_SPEC] * n + [VMEM_SPEC],
        out_specs=[VMEM_SPEC] * 2,
        scratch_shapes=[pltpu.VMEM((rows, n * wide), jnp.bfloat16), pltpu.SemaphoreType.DMA((n,))],
        compiler_params=pltpu.CompilerParams(vmem_limit_bytes=SCOPED),
        cost_estimate=pl.CostEstimate(
            flops=2 * rows * n_docs * n * wide, bytes_accessed=(rows + n_docs) * n * wide * 2, transcendentals=0
        ),
    )(blocks, *pieces, docs)


def score_next_kernel(n, start, *refs):
    pieces, (columns, before, out, packed, sems) = refs[:n], refs[n:]
    rows = packed_rows(pieces, packed, sems)
    for j in range(columns.shape[0] // STEP):
        at = slice(j * STEP, (j + 1) * STEP)
        out[:, at] = before[:, at] + product(rows, columns[at, start : start + rows.shape[1]])


def score_next(start, pieces, columns, before):
    rows, wide = pieces[0].shape
    n_docs = columns.shape[0]
    n = len(pieces)
    return pl.pallas_call(
        functools.partial(score_next_kernel, n, start),
        out_shape=jax.ShapeDtypeStruct((rows, n_docs), jnp.float32),
        in_specs=[ANY_SPEC] * n + [VMEM_SPEC] * 2,
        out_specs=VMEM_SPEC,
        scratch_shapes=[pltpu.VMEM((rows, n * wide), jnp.bfloat16), pltpu.SemaphoreType.DMA((n,))],
        input_output_aliases={n + 1: 0},
        compiler_params=pltpu.CompilerParams(vmem_limit_bytes=SCOPED),
        cost_estimate=pl.CostEstimate(
            flops=2 * rows * n_docs * n * wide, bytes_accessed=(rows + n_docs) * n * wide * 2, transcendentals=0
        ),
    )(*pieces, columns, before)


def score_chunk_kernel(n, start, chunk, *refs):
    pieces, (columns, before, out, packed, sems) = refs[:n], refs[n:]
    tall = out.shape[0]
    mine = pl.ds(chunk * tall, tall)
    rows = packed_rows([piece.at[mine, :] for piece in pieces], packed, sems)
    for j in range(columns.shape[0] // STEP):
        at = slice(j * STEP, (j + 1) * STEP)
        out[:, at] = before[mine, at] + product(rows, columns[at, start : start + rows.shape[1]])


def score_chunk(start, pieces, columns, before, chunk):
    rows, wide = pieces[0].shape[0] // CHUNKS, pieces[0].shape[1]
    n_docs = columns.shape[0]
    n = len(pieces)
    return pl.pallas_call(
        functools.partial(score_chunk_kernel, n, start, chunk),
        out_shape=jax.ShapeDtypeStruct((rows, n_docs), jnp.float32),
        in_specs=[ANY_SPEC] * n + [VMEM_SPEC] * 2,
        out_specs=VMEM_SPEC,
        scratch_shapes=[pltpu.VMEM((rows, n * wide), jnp.bfloat16), pltpu.SemaphoreType.DMA((n,))],
        compiler_params=pltpu.CompilerParams(vmem_limit_bytes=SCOPED),
        cost_estimate=pl.CostEstimate(
            flops=2 * rows * n_docs * n * wide, bytes_accessed=(rows + n_docs) * n * wide * 2, transcendentals=0
        ),
    )(*pieces, columns, before)


def score_last_kernel(n, start, chunk, *refs):
    pieces, columns, before, outs = refs[:n], refs[n], refs[n + 1], refs[n + 2 :]
    tall = before.shape[0]
    mine = slice(chunk * tall, (chunk + 1) * tall)
    rows = jnp.concatenate([piece[mine, :] for piece in pieces], axis=1)
    for j in range(columns.shape[0] // STEP):
        at = slice(j * STEP, (j + 1) * STEP)
        part = before[:, at] + product(rows, columns[at, start:])
        top = 0
        for out in outs:
            out[:, at] = part[top : top + out.shape[0], :].astype(out.dtype)
            top += out.shape[0]


def score_last(start, pieces, columns, before, chunk, heights):
    rows, wide = pieces[0].shape
    n_docs = columns.shape[0]
    n = len(pieces)
    shapes = [
        jax.ShapeDtypeStruct((tall, n_docs), jnp.bfloat16 if i else jnp.float32) for i, tall in enumerate(heights)
    ]
    return pl.pallas_call(
        functools.partial(score_last_kernel, n, start, chunk),
        out_shape=shapes,
        in_specs=[VMEM_SPEC] * (n + 2),
        out_specs=[VMEM_SPEC] * len(shapes),
        compiler_params=pltpu.CompilerParams(vmem_limit_bytes=SCOPED),
        cost_estimate=pl.CostEstimate(
            flops=2 * rows // CHUNKS * n_docs * n * wide, bytes_accessed=2**23, transcendentals=0
        ),
    )(*pieces, columns, before)


def exchange_y(own, ahead, far, back):
    steps = ((ahead, 1), (back, -1), (far, 2))
    return [own] + [move(part, group_perm(0, dy), "group") for part, dy in steps]


def exchange_h(own, other):
    return [own, move(other, group_perm(1, 0), "group")]


def added(parts):
    return sum(part.astype(jnp.float32) for part in parts)


def parts_of(rows, count):
    tall = rows.shape[0] // count
    return [rows[i * tall : (i + 1) * tall].astype(jnp.bfloat16 if i else jnp.float32) for i in range(count)]


def local(queries, precond, documents):
    rows, feat = queries.shape
    h, y = lax.axis_index("group") // NY, lax.axis_index("group") % NY
    chips, cores = places()
    dy, dh = (chips % NY - y + NY) % NY, (chips // NY - h + NH) % NH
    place = jnp.stack([(dh * NY + dy) * NC + cores, GROUP * NC + (dy * NH + dh) * NC + cores])
    blocks = chips * NC + cores
    early = NC * STAGES[1][1]
    half = NC * STAGES[0][1]

    one = lax.optimization_barrier(first_stage(queries))
    weights = lax.all_to_all(column_blocks(precond, CHIPS * NC), "corpus", 0, 0, tiled=True).reshape(feat, -1)
    two = second_stage(*one)
    three = third_stage(*two)
    conditioned, weights = condition(place[:, :early], with_core(one + two), weights)
    three, conditioned = lax.optimization_barrier((three, conditioned))
    conditioned = condition_rest(place[:, early:], with_core(three), weights, conditioned)

    wide = conditioned.shape[1]
    one = first_stage(conditioned)
    scores, columns = score_first(blocks, with_core(one[:1]), documents)
    one[1:3], scores = lax.optimization_barrier((one[1:3], scores))
    two = second_stage(*one)
    scores = score_next(0, with_core(one[1:]), columns, scores)
    two[0], scores = lax.optimization_barrier((two[0], scores))
    three = third_stage(*two)
    scores, *_ = lax.optimization_barrier((scores, three[0]))
    after, start = (half - NC) * wide, (early - NC) * wide
    middle, pieces = with_core(two), with_core(three)
    tall = conditioned.shape[0] // CHUNKS
    first = score_chunk(after, middle, columns, scores, 0)
    first = score_last(start, pieces, columns, first, 0, [tall // NH] * NH)
    scores, *_ = lax.optimization_barrier((scores, first[0]))
    part, less = tall // NY, tall // GROUP
    second = score_chunk(after, middle, columns, scores, 1)
    own, ahead, far, across, back = score_last(start, pieces, columns, second, 1, [part, part, less, less, part])
    go = functools.partial(move, axis="group")
    near = [own, go(ahead, group_perm(0, 1)), go(back, group_perm(0, -1))]
    distant = [go(far, group_perm(0, 2)), go(across, group_perm(1, 2))]
    first, near = lax.optimization_barrier((exchange_h(*first), near))
    first = added(exchange_y(*parts_of(added(first), NY)))
    second = added(exchange_h(*parts_of(added(near), NH)) + distant)
    totals = [total.reshape(NC, rows // CHUNKS, -1) for total in (first, second)]
    scores = jnp.concatenate(totals, axis=1).reshape(NC * rows, -1)
    return scores / jnp.sqrt(jnp.float32(GROUP * feat))


def solution(mesh):
    placed = (P("corpus", "group"), P("group", "corpus", None), P("corpus", "group"))
    return jax.shard_map(
        local, mesh=mesh, in_specs=placed, out_specs=P("group", "corpus"), check_vma=False
    )
```

```python
import functools

import jax
import jax.numpy as jnp
from jax import lax
from jax.experimental import pallas as pl
from jax.experimental.pallas import tpu as pltpu
from jax.sharding import PartitionSpec as P

NZ, NX, NC, NH, NY = 4, 2, 2, 2, 4
CHIPS = NZ * NX
GROUP = NH * NY
ROLES = ((0, 0), (0, 1), (-1, 0), (1, 0), (-1, 1), (2, 0), (1, 1), (2, 1))
STAGES = ((0, 4), (4, 7), (7, 8))


def corpus_perm(move):
    pairs = []
    for z in range(NZ):
        for x in range(NX):
            for c in range(NC):
                dz, dx, dc = move(1 - 2 * c)
                to = ((z + dz) % NZ, (x + dx) % NX, (c + dc) % NC)
                pairs.append(((z * NX + x) * NC + c, (to[0] * NX + to[1]) * NC + to[2]))
    return pairs


def group_perm(dh, dy):
    return [(h * NY + y, (h + dh) % NH * NY + (y + dy) % NY) for h in range(NH) for y in range(NY)]


AHEAD = corpus_perm(lambda d: (d, 0, 0))
BACK = corpus_perm(lambda d: (-d, 0, 0))
CROSS = corpus_perm(lambda d: (0, 1, 0))
CORE = corpus_perm(lambda d: (0, 0, 1))


CHUNKS = 2
STEP = 512
SCOPED = 12 * 2**20
ANY_SPEC = pl.BlockSpec(memory_space=pl.ANY)
HBM_SPEC = pl.BlockSpec(memory_space=pltpu.HBM)
VMEM_SPEC = pl.BlockSpec(memory_space=pltpu.VMEM)
SMEM_SPEC = pl.BlockSpec(memory_space=pltpu.SMEM)


def move(piece, perm, axis="corpus"):
    return lax.ppermute(piece, axis, perm)


def with_core(pieces):
    return [p for piece in pieces for p in (piece, move(piece, CORE))]


def first_stage(own):
    return [own, move(own, CROSS), move(own, AHEAD), move(own, BACK)]


def second_stage(own, cross, behind, ahead):
    return [move(cross, AHEAD), move(behind, AHEAD), move(ahead, CROSS)]


def third_stage(cross_behind, far, cross_ahead):
    return [move(cross_behind, AHEAD)]


def places():
    place = lax.axis_index("corpus")
    z, x, core = place // (NX * NC), place // NC % NX, place % NC
    chips, cores = [], []
    for dz, dx in ROLES:
        for c in (core, 1 - core):
            chips.append(((z + dz * (1 - 2 * c) + NZ) % NZ) * NX + (x + dx) % NX)
            cores.append(c)
    return jnp.stack(chips), jnp.stack(cores)


def blocks_kernel(weights, out, sems):
    wide = out.shape[2]
    copies = [
        pltpu.make_async_copy(weights.at[0, :, pl.ds(i * wide, wide)], out.at[i], sems.at[i])
        for i in range(out.shape[0])
    ]
    for copy in copies:
        copy.start()
    for copy in copies:
        copy.wait()


def column_blocks(weights, count):
    _, rows, columns = weights.shape
    return pl.pallas_call(
        blocks_kernel,
        out_shape=jax.ShapeDtypeStruct((count, rows, columns // count), weights.dtype),
        in_specs=[HBM_SPEC],
        out_specs=VMEM_SPEC,
        scratch_shapes=[pltpu.SemaphoreType.DMA((count,))],
    )(weights)


def condition_kernel(n, place, *refs):
    pieces, weights, (out, held, rows, sems) = refs[:n], refs[n], refs[n + 1 :]
    tall = pieces[0].shape[0]
    loads = [pltpu.make_async_copy(weights, held, sems.at[n])]
    for i, piece in enumerate(pieces):
        loads.append(pltpu.make_async_copy(piece, rows.at[pl.ds(i * tall, tall), :], sems.at[i]))
    for load in loads:
        load.start()
    for load in loads:
        load.wait()
    done = jnp.dot(rows[...], held[...], preferred_element_type=jnp.float32).astype(jnp.bfloat16)
    to_places(place, n, tall, done, out)


def to_places(place, n, tall, done, out):
    few = tall // CHUNKS
    for i in range(n):
        for k in range(CHUNKS):
            to = pl.multiple_of(place[k, i] * few, few)
            out[pl.ds(to, few), :] = done[i * tall + k * few : i * tall + (k + 1) * few, :]


def condition(place, pieces, weights):
    tall, depth = pieces[0].shape
    wide = weights.shape[1]
    n = len(pieces)
    return pl.pallas_call(
        functools.partial(condition_kernel, n),
        out_shape=[
            jax.ShapeDtypeStruct((CHIPS * NC * tall, wide), jnp.bfloat16),
            jax.ShapeDtypeStruct(weights.shape, weights.dtype),
        ],
        in_specs=[SMEM_SPEC] + [ANY_SPEC] * n + [HBM_SPEC],
        out_specs=[VMEM_SPEC] * 2,
        scratch_shapes=[pltpu.VMEM((n * tall, depth), jnp.bfloat16), pltpu.SemaphoreType.DMA((n + 1,))],
        compiler_params=pltpu.CompilerParams(vmem_limit_bytes=52 * 2**20),
        cost_estimate=pl.CostEstimate(
            flops=2 * n * tall * depth * wide, bytes_accessed=(n * tall + wide) * depth * 2, transcendentals=0
        ),
    )(place, *pieces, weights)


def condition_rest_kernel(n, place, *refs):
    pieces, (weights, into, out) = refs[:n], refs[n:]
    tall = pieces[0].shape[0]
    rows = jnp.concatenate([piece[...] for piece in pieces], axis=0)
    done = jnp.dot(rows, weights[...], preferred_element_type=jnp.float32).astype(jnp.bfloat16)
    out[...] = into[...]
    to_places(place, n, tall, done, out)


def condition_rest(place, pieces, weights, into):
    tall, depth = pieces[0].shape
    n = len(pieces)
    return pl.pallas_call(
        functools.partial(condition_rest_kernel, n),
        out_shape=jax.ShapeDtypeStruct(into.shape, into.dtype),
        in_specs=[SMEM_SPEC] + [VMEM_SPEC] * (n + 2),
        out_specs=VMEM_SPEC,
        compiler_params=pltpu.CompilerParams(vmem_limit_bytes=24 * 2**20),
        cost_estimate=pl.CostEstimate(
            flops=2 * n * tall * depth * into.shape[1], bytes_accessed=2**22, transcendentals=0
        ),
    )(place, *pieces, weights, into)


def packed_rows(pieces, packed, sems):
    wide = pieces[0].shape[1]
    copies = [
        pltpu.make_async_copy(piece, packed.at[:, pl.ds(i * wide, wide)], sems.at[i])
        for i, piece in enumerate(pieces)
    ]
    for copy in copies:
        copy.start()
    for copy in copies:
        copy.wait()
    return packed[...]


def product(rows, columns):
    return lax.dot_general(rows, columns, (((1,), (1,)), ((), ())), preferred_element_type=jnp.float32)


def score_first_kernel(n, blocks, *refs):
    pieces, (docs, out, rest, packed, sems) = refs[:n], refs[n:]
    wide = pieces[0].shape[1]
    rows = packed_rows(pieces, packed, sems)
    for j in range(docs.shape[0] // STEP):
        at = slice(j * STEP, (j + 1) * STEP)
        columns = [
            docs[at, pl.ds(pl.multiple_of(blocks[i] * wide, wide), wide)] for i in range(docs.shape[1] // wide)
        ]
        out[:, at] = product(rows, jnp.concatenate(columns[:n], axis=1))
        rest[at, :] = jnp.concatenate(columns[n:], axis=1)


def score_first(blocks, pieces, docs):
    rows, wide = pieces[0].shape
    n_docs, depth = docs.shape
    n = len(pieces)
    return pl.pallas_call(
        functools.partial(score_first_kernel, n),
        out_shape=[
            jax.ShapeDtypeStruct((rows, n_docs), jnp.float32),
            jax.ShapeDtypeStruct((n_docs, depth - n * wide), docs.dtype),
        ],
        in_specs=[SMEM_SPEC] + [ANY_SPEC] * n + [VMEM_SPEC],
        out_specs=[VMEM_SPEC] * 2,
        scratch_shapes=[pltpu.VMEM((rows, n * wide), jnp.bfloat16), pltpu.SemaphoreType.DMA((n,))],
        compiler_params=pltpu.CompilerParams(vmem_limit_bytes=SCOPED),
        cost_estimate=pl.CostEstimate(
            flops=2 * rows * n_docs * n * wide, bytes_accessed=(rows + n_docs) * n * wide * 2, transcendentals=0
        ),
    )(blocks, *pieces, docs)


def score_next_kernel(n, start, *refs):
    pieces, (columns, before, out, packed, sems) = refs[:n], refs[n:]
    rows = packed_rows(pieces, packed, sems)
    for j in range(columns.shape[0] // STEP):
        at = slice(j * STEP, (j + 1) * STEP)
        out[:, at] = before[:, at] + product(rows, columns[at, start : start + rows.shape[1]])


def score_next(start, pieces, columns, before):
    rows, wide = pieces[0].shape
    n_docs = columns.shape[0]
    n = len(pieces)
    return pl.pallas_call(
        functools.partial(score_next_kernel, n, start),
        out_shape=jax.ShapeDtypeStruct((rows, n_docs), jnp.float32),
        in_specs=[ANY_SPEC] * n + [VMEM_SPEC] * 2,
        out_specs=VMEM_SPEC,
        scratch_shapes=[pltpu.VMEM((rows, n * wide), jnp.bfloat16), pltpu.SemaphoreType.DMA((n,))],
        input_output_aliases={n + 1: 0},
        compiler_params=pltpu.CompilerParams(vmem_limit_bytes=SCOPED),
        cost_estimate=pl.CostEstimate(
            flops=2 * rows * n_docs * n * wide, bytes_accessed=(rows + n_docs) * n * wide * 2, transcendentals=0
        ),
    )(*pieces, columns, before)


def score_chunk_kernel(n, start, chunk, *refs):
    pieces, (columns, before, out, packed, sems) = refs[:n], refs[n:]
    tall = out.shape[0]
    mine = pl.ds(chunk * tall, tall)
    rows = packed_rows([piece.at[mine, :] for piece in pieces], packed, sems)
    for j in range(columns.shape[0] // STEP):
        at = slice(j * STEP, (j + 1) * STEP)
        out[:, at] = before[mine, at] + product(rows, columns[at, start : start + rows.shape[1]])


def score_chunk(start, pieces, columns, before, chunk):
    rows, wide = pieces[0].shape[0] // CHUNKS, pieces[0].shape[1]
    n_docs = columns.shape[0]
    n = len(pieces)
    return pl.pallas_call(
        functools.partial(score_chunk_kernel, n, start, chunk),
        out_shape=jax.ShapeDtypeStruct((rows, n_docs), jnp.float32),
        in_specs=[ANY_SPEC] * n + [VMEM_SPEC] * 2,
        out_specs=VMEM_SPEC,
        scratch_shapes=[pltpu.VMEM((rows, n * wide), jnp.bfloat16), pltpu.SemaphoreType.DMA((n,))],
        compiler_params=pltpu.CompilerParams(vmem_limit_bytes=SCOPED),
        cost_estimate=pl.CostEstimate(
            flops=2 * rows * n_docs * n * wide, bytes_accessed=(rows + n_docs) * n * wide * 2, transcendentals=0
        ),
    )(*pieces, columns, before)


def score_last_kernel(n, start, chunk, *refs):
    pieces, columns, before, outs = refs[:n], refs[n], refs[n + 1], refs[n + 2 :]
    tall = before.shape[0]
    mine = slice(chunk * tall, (chunk + 1) * tall)
    rows = jnp.concatenate([piece[mine, :] for piece in pieces], axis=1)
    for j in range(columns.shape[0] // STEP):
        at = slice(j * STEP, (j + 1) * STEP)
        part = before[:, at] + product(rows, columns[at, start:])
        top = 0
        for out in outs:
            out[:, at] = part[top : top + out.shape[0], :].astype(out.dtype)
            top += out.shape[0]


def score_last(start, pieces, columns, before, chunk, heights):
    rows, wide = pieces[0].shape
    n_docs = columns.shape[0]
    n = len(pieces)
    shapes = [
        jax.ShapeDtypeStruct((tall, n_docs), jnp.bfloat16 if i else jnp.float32) for i, tall in enumerate(heights)
    ]
    return pl.pallas_call(
        functools.partial(score_last_kernel, n, start, chunk),
        out_shape=shapes,
        in_specs=[VMEM_SPEC] * (n + 2),
        out_specs=[VMEM_SPEC] * len(shapes),
        compiler_params=pltpu.CompilerParams(vmem_limit_bytes=SCOPED),
        cost_estimate=pl.CostEstimate(
            flops=2 * rows // CHUNKS * n_docs * n * wide, bytes_accessed=2**23, transcendentals=0
        ),
    )(*pieces, columns, before)


def exchange_y(own, ahead, far, back):
    steps = ((ahead, 1), (back, -1), (far, 2))
    return [own] + [move(part, group_perm(0, dy), "group") for part, dy in steps]


def exchange_h(own, other):
    return [own, move(other, group_perm(1, 0), "group")]


def added(parts):
    return sum(part.astype(jnp.float32) for part in parts)


def parts_of(rows, count):
    tall = rows.shape[0] // count
    return [rows[i * tall : (i + 1) * tall].astype(jnp.bfloat16 if i else jnp.float32) for i in range(count)]


def local(queries, precond, documents):
    rows, feat = queries.shape
    h, y = lax.axis_index("group") // NY, lax.axis_index("group") % NY
    chips, cores = places()
    dy, dh = (chips % NY - y + NY) % NY, (chips // NY - h + NH) % NH
    place = jnp.stack([(dh * NY + dy) * NC + cores, GROUP * NC + (dy * NH + dh) * NC + cores])
    blocks = chips * NC + cores
    early = NC * STAGES[1][1]
    half = NC * STAGES[0][1]

    one = lax.optimization_barrier(first_stage(queries))
    weights = lax.all_to_all(column_blocks(precond, CHIPS * NC), "corpus", 0, 0, tiled=True).reshape(feat, -1)
    two = second_stage(*one)
    three = third_stage(*two)
    conditioned, weights = condition(place[:, :early], with_core(one + two), weights)
    three, conditioned = lax.optimization_barrier((three, conditioned))
    conditioned = condition_rest(place[:, early:], with_core(three), weights, conditioned)

    wide = conditioned.shape[1]
    one = first_stage(conditioned)
    scores, columns = score_first(blocks, with_core(one[:1]), documents)
    one[1:3], scores = lax.optimization_barrier((one[1:3], scores))
    two = second_stage(*one)
    scores = score_next(0, with_core(one[1:]), columns, scores)
    two[0], scores = lax.optimization_barrier((two[0], scores))
    three = third_stage(*two)
    held, *_ = lax.optimization_barrier((scores, three[0]))
    after, start = (half - NC) * wide, (early - NC) * wide
    middle, pieces = with_core(two), with_core(three)
    tall = conditioned.shape[0] // CHUNKS
    first = score_chunk(after, middle, columns, held, 0)
    first = score_last(start, pieces, columns, first, 0, [tall // NH] * NH)
    part, less = tall // NY, tall // GROUP
    second = score_chunk(after, middle, columns, scores, 1)
    second, *_ = lax.optimization_barrier((second, first[0]))
    own, ahead, far, across, back = score_last(start, pieces, columns, second, 1, [part, part, less, less, part])
    go = functools.partial(move, axis="group")
    near = [own, go(ahead, group_perm(0, 1)), go(back, group_perm(0, -1))]
    distant = [go(far, group_perm(0, 2)), go(across, group_perm(1, 2))]
    first, near = lax.optimization_barrier((exchange_h(*first), near))
    first = added(exchange_y(*parts_of(added(first), NY)))
    second = added(exchange_h(*parts_of(added(near), NH)) + distant)
    totals = [total.reshape(NC, rows // CHUNKS, -1) for total in (first, second)]
    scores = jnp.concatenate(totals, axis=1).reshape(NC * rows, -1)
    return scores / jnp.sqrt(jnp.float32(GROUP * feat))


def solution(mesh):
    placed = (P("corpus", "group"), P("group", "corpus", None), P("corpus", "group"))
    return jax.shard_map(
        local, mesh=mesh, in_specs=placed, out_specs=P("group", "corpus"), check_vma=False
    )
```
